128 devices in a mesh: harm: 16 (over x, z_hi, core), mode: 8 (over y, z_lo).
Axes of the slice: x: 4, y: 4, z: 4 (z_hi: 2, z_lo: 2; z = z_hi * 2 + z_lo), core: 2. Of those that a mesh axis runs over, the one named last changes fastest.
Arguments:
- mode_vectors: float32 [49152, 1024], P('harm', 'mode'), may hold values from -0.09375 to 0.09375
- weights: float32 [49152, 1024], P('harm', 'mode'), may hold values from -0.1875 to 0.1875
- cotangent: float32 [49152, 1024], P('harm', 'mode'), may hold values from -6 to 6
- eigenvalues: float32 [1024], replicated, may hold values from 0 to 4
- eigen_cotangent: float32 [1024], replicated, may hold values from -6 to 6
- slab_rows: int32 [4096], replicated, may hold values from 0 to 49151, as said below
Outputs:
- slab: float32 [4096, 49152], P('mode', 'harm')
The draws below stay inside these ranges and needn't reach their ends.
Inputs may be any that keep to these rules, and one draw needn't show every extreme that they name: `slab_rows`: each block of 3072 consecutive harmonics (0 to 3071, 3072 to 6143 and so on) holds exactly 256 of the slab rows.
All inputs are finite; a program needn't handle non-finite values.
Results may differ from the reference program's by a relative error of at most 0.0001.
Values sent between devices are 32-bit elements; how exact they have to be, the bound alone decides.
No kernel may reach another device: no remote copies, remote signals or barrier semaphores. Data moves between devices by JAX's collectives and lax.ppermute only.
A program may use at most 128 MiB of HBM per device.

```python
import jax
import jax.numpy as jnp
from jax import lax

H = 49152
K = 1024
R = 4096
HB = 3072
RB = 256


def draw_slab_rows(key, part):
    first_key = jax.random.fold_in(key, 11)
    second_key = jax.random.fold_in(key, 23)
    block_ids = jnp.arange(R, dtype=jnp.int32) // RB
    within = jax.random.randint(first_key, (R,), 0, HB, dtype=jnp.int32)
    values = block_ids * HB + within
    order = jax.random.permutation(second_key, R)
    return jnp.take(values, order, axis=0).astype(jnp.int32)


def levels(key, extent, cuts, low, top_value):
    def one(dim, parts):
        draws = jax.random.uniform(jax.random.fold_in(jax.random.fold_in(key, 6), dim), (parts,), jnp.float32, low / len(cuts), top_value / len(cuts))
        return jnp.repeat(jnp.exp(draws), extent[dim] // parts).reshape((-1,) + (1,) * (len(extent) - dim - 1))

    gain = one(*cuts[0])
    for cut in cuts[1:]:
        gain = gain * one(*cut)
    return gain


def bell_draw(own_key, dims, scale, most, cuts=(), kind=jnp.bfloat16):
    loudness = levels(own_key, dims, cuts, -0.22, 0.18) if cuts else 1.0
    result = jax.random.normal(own_key, dims, jnp.float32) * scale * loudness
    return jnp.minimum(jnp.maximum(result, -most), most).astype(kind)


def setup_inputs(seed: int = 0) -> dict:
    seeds = jax.random.split(jax.random.key(seed), 7)
    return {
        "mode_vectors": bell_draw(seeds[0], (H, K), (4 * K) ** -0.5, 0.09375, ((0, 16), (1, 8)), jnp.float32),
        "weights": bell_draw(seeds[1], (H, K), K ** -0.5, 0.1875, ((0, 16), (1, 8)), jnp.float32),
        "cotangent": bell_draw(seeds[2], (H, K), 1.0, 6.0, ((0, 16), (1, 8)), jnp.float32),
        "eigenvalues": jnp.clip(jax.random.uniform(seeds[3], (K,), jnp.float32, 0.0, 4.0), 0.0, 4.0),
        "eigen_cotangent": bell_draw(seeds[4], (K,), 1.0, 6.0, (), jnp.float32),
        "slab_rows": draw_slab_rows(jax.random.fold_in(seeds[6], 71), 0),
    }


regular = 0.01


def reference(mode_vectors, weights, cotangent, eigenvalues, eigen_cotangent, slab_rows):
    highest = lax.Precision.HIGHEST
    gram = jnp.dot(mode_vectors.T, cotangent, precision=highest, preferred_element_type=jnp.float32)
    differ = eigenvalues[None, :] - eigenvalues[:, None]
    factor = differ / (differ * differ + regular)
    weighted = factor * gram + jnp.diag(eigen_cotangent)
    picked = jnp.take(weights, slab_rows.astype(jnp.int32), axis=0)
    z_rows = jnp.dot(picked, weighted, precision=highest, preferred_element_type=jnp.float32)
    return jnp.dot(z_rows, mode_vectors.T, precision=highest, preferred_element_type=jnp.float32)
```

```python
import jax
import jax.numpy as jnp
from jax import lax
from jax.experimental import pallas as pl
from jax.experimental.pallas import tpu as pltpu
from jax.sharding import Mesh
from jax.sharding import PartitionSpec as P

HARM = ("x", "zh", "c")
MODE = ("y", "zl")
SIZES = {"x": 4, "zh": 2, "c": 2, "y": 4, "zl": 2}
regular = 0.01
TILE = 256
VMEM = 60 * 1024 * 1024


def shifted(array, axis, step):
    n = SIZES[axis]
    return lax.ppermute(array, axis, [(i, (i + step) % n) for i in range(n)])


def pick(parts, number):
    return lax.dynamic_index_in_dim(parts, number, 0, keepdims=False)


def slot_of(offset):
    return jnp.where(offset == 0, 0, jnp.where(offset == 3, 1, jnp.where(offset == 1, 2, 3)))


def ring_parts(array, axis):
    return jnp.stack([array, shifted(array, axis, 1), shifted(array, axis, -1), shifted(array, axis, 2)])


def split(value):
    high = value.astype(jnp.bfloat16)
    low = (value - high.astype(jnp.float32)).astype(jnp.bfloat16)
    return high, low


def three_pass(a, b, dims):
    a_high, a_low = a
    b_high, b_low = b
    def dot(p, q):
        return lax.dot_general(p, q, (dims, ((), ())), preferred_element_type=jnp.float32)
    return dot(a_high, b_high) + dot(a_high, b_low) + dot(a_low, b_high)


def gram_part(cots, blocks):
    rows = cots[0].shape[0]
    tile = 512
    steps = rows // tile
    flat, plan, firsts = [], [], []
    for block in blocks:
        first, pieces = 0, []
        for piece in block:
            count = piece.shape[0] // tile
            pieces.append((len(flat), first, count))
            flat.append(piece)
            firsts.append((first, count))
            first += count
        plan.append(pieces)

    def body(*refs):
        cot_refs, piece_refs, out = refs[: len(cots)], refs[len(cots) : -1], refs[-1]
        step = pl.program_id(0)

        @pl.when(step == 0)
        def _():
            out[...] = jnp.zeros_like(out)

        cot = split(jnp.concatenate([r[...] for r in cot_refs], axis=1))
        found = []
        for pieces in plan:
            value = piece_refs[pieces[0][0]][...]
            for index, first, _ in pieces[1:]:
                value = jnp.where(step >= first, piece_refs[index][...], value)
            found.append(value)
        block = split(jnp.concatenate(found, axis=1) if len(found) > 1 else found[0])
        out[...] += three_pass(cot, block, ((0,), (0,)))

    def spec(first, count):
        return pl.BlockSpec((tile, 128), lambda i: (jnp.clip(i - first, 0, count - 1), 0))

    width, cols = 128 * len(cots), 128 * len(blocks)
    return pl.pallas_call(
        body,
        grid=(steps,),
        in_specs=[spec(0, steps) for _ in cots] + [spec(f, n) for f, n in firsts],
        out_specs=pl.BlockSpec((width, cols), lambda i: (0, 0)),
        out_shape=jax.ShapeDtypeStruct((width, cols), jnp.float32),
        compiler_params=pltpu.CompilerParams(vmem_limit_bytes=VMEM),
        cost_estimate=pl.CostEstimate(
            flops=6 * rows * width * cols, bytes_accessed=4 * rows * (width + cols), transcendentals=0
        ),
    )(*cots, *flat)


def slab_part(z, blocks):
    total = sum(p.shape[0] for p in blocks[0])
    steps = total // TILE
    depth = z.shape[1]
    flat, plan, firsts = [], [], []
    for block in blocks:
        first, pieces = 0, []
        for piece in block:
            count = piece.shape[0] // TILE
            pieces.append((len(flat), first, count))
            flat.append(piece)
            firsts.append((first, count))
            first += count
        plan.append(pieces)

    def body(z_ref, *refs):
        piece_refs, out, z_high, z_low = refs[:-3], refs[-3], refs[-2], refs[-1]
        step = pl.program_id(0)

        @pl.when(step == 0)
        def _():
            z_high[...], z_low[...] = split(z_ref[...])

        found = []
        for pieces in plan:
            value = piece_refs[pieces[0][0]][...]
            for index, first, _ in pieces[1:]:
                value = jnp.where(step >= first, piece_refs[index][...], value)
            found.append(value)
        x = split(jnp.concatenate(found, axis=1))
        out[...] = three_pass((z_high[...], z_low[...]), x, ((1,), (1,)))

    def spec(first, count):
        return pl.BlockSpec((TILE, 128), lambda i: (jnp.clip(i - first, 0, count - 1), 0))

    return pl.pallas_call(
        body,
        grid=(steps,),
        in_specs=[pl.BlockSpec(z.shape, lambda i: (0, 0))] + [spec(f, n) for f, n in firsts],
        out_specs=pl.BlockSpec((z.shape[0], TILE), lambda i: (0, i)),
        out_shape=jax.ShapeDtypeStruct((z.shape[0], total), jnp.float32),
        scratch_shapes=[pltpu.VMEM(z.shape, jnp.bfloat16), pltpu.VMEM(z.shape, jnp.bfloat16)],
        compiler_params=pltpu.CompilerParams(vmem_limit_bytes=VMEM),
        cost_estimate=pl.CostEstimate(
            flops=6 * total * z.shape[0] * depth,
            bytes_accessed=4 * (total * depth + total * z.shape[0]),
            transcendentals=0,
        ),
    )(z, *flat)


def slab_weights(weights, slab_rows, x, zh, c, y, zl):
    height = weights.shape[0]
    total = slab_rows.shape[0]
    count = total // 16
    harm = (x * 2 + zh) * 2 + c
    arranged = jnp.argsort(slab_rows // height, stable=True).astype(jnp.int32)
    place = jnp.argsort(arranged).astype(jnp.int32)
    own_slots = lax.dynamic_slice_in_dim(arranged, harm * count, count)
    own = jnp.take(slab_rows, own_slots, axis=0, mode="clip") - harm * height
    rows = jnp.take(weights, own, axis=0, mode="clip")
    pair = jnp.stack([rows, shifted(rows, "zh", 1)])
    ring = ring_parts(pair, "x")
    every = jnp.stack([ring, shifted(ring, "c", 1)])
    every = every.reshape(-1, 128)
    share = total // 8 // 8
    wanted = lax.dynamic_slice_in_dim(place.reshape(8, 8, share), x * 2 + c, 1, axis=1).reshape(-1)
    source, row = wanted // count, wanted % count
    source_x, source_zh, source_c = source // 4, (source // 2) % 2, source % 2
    held = (
        ((source_c != c) * 4 + slot_of((source_x - x) % 4)) * 2 + (source_zh != zh)
    ) * count + row
    chosen = jnp.take(every, held, axis=0, mode="clip").reshape(8, share, 128)
    came = lax.all_to_all(chosen, MODE, 0, 0, tiled=True).reshape(4, 2, share, 128)
    came = jnp.where(zl == 0, came, came[:, ::-1])
    came = came.transpose(2, 1, 0, 3).reshape(share, 1024)
    return lax.all_gather(came, ("x", "c"), axis=0, tiled=True)


def local(mode_vectors, weights, cotangent, eigenvalues, eigen_cotangent, slab_rows):
    x, zh, c, y, zl = (lax.axis_index(a) for a in ("x", "zh", "c", "y", "zl"))
    rows = mode_vectors.shape[0]
    half = rows // 2
    cut = rows * 3 // 4
    mid = TILE * ((cut // 2) // TILE)

    below = shifted(mode_vectors, "y", 1)
    above = shifted(mode_vectors, "y", -1)
    other_cot = shifted(cotangent, "zl", 1)
    far = [shifted(below[:half], "y", 1), shifted(above[half:], "y", -1)]
    other_a = shifted(mode_vectors[:mid], "zl", 1)
    other_b = shifted(mode_vectors[mid:cut], "zl", 1)
    other_c = shifted(mode_vectors[cut:], "zl", 1)
    other_below_a = shifted(other_a, "y", 1)
    other_above_a = shifted(other_a, "y", -1)
    other_below_b = shifted(other_b, "y", 1)
    other_above_b = shifted(other_b, "y", -1)
    other_far = [shifted(other_below_a, "y", 1), shifted(other_above_b, "y", -1)]
    other_below_c = shifted(below[cut:], "zl", 1)
    other_above_c = shifted(above[cut:], "zl", 1)
    other_far_c = shifted(far[1][cut - half :], "zl", 1)

    picked = slab_weights(weights, slab_rows, x, zh, c, y, zl)

    near = gram_part([cotangent, other_cot], [[mode_vectors], [below], [above]])
    last = gram_part([cotangent, other_cot], [far])
    gram = jnp.concatenate([near, last], axis=1)
    gram = jnp.where(zl == 0, gram, jnp.roll(gram, 128, axis=0))
    gram = gram.reshape(4, 2, 32, 512)
    core = lax.dynamic_index_in_dim(gram, c, 1, keepdims=False) + shifted(
        lax.dynamic_index_in_dim(gram, 1 - c, 1, keepdims=False), "c", 1
    )
    total = (
        pick(core, x)
        + shifted(pick(core, (x + 1) % 4), "x", 1)
        + shifted(pick(core, (x + 3) % 4), "x", -1)
        + shifted(pick(core, (x + 2) % 4), "x", 2)
    )
    total = total + shifted(total, "zh", 1)
    parts = total.reshape(32, 4, 128)
    parts = jnp.stack(
        [lax.dynamic_index_in_dim(parts, slot_of((k - y) % 4), 1, keepdims=False) for k in range(4)], axis=1
    )
    j_first = (y * 2 + x // 2) * 128 + ((x % 2) * 2 + c) * 32
    eigen_j = lax.dynamic_slice_in_dim(eigenvalues, j_first, 32)
    slope_j = lax.dynamic_slice_in_dim(eigen_cotangent, j_first, 32)
    eigen_i = lax.dynamic_index_in_dim(eigenvalues.reshape(4, 2, 128), zl, 1, keepdims=False)
    differ = eigen_j[:, None, None] - eigen_i[None]
    factor = differ / (differ * differ + regular)
    shape = parts.shape
    j_ids = j_first + lax.broadcasted_iota(jnp.int32, shape, 0)
    i_ids = (lax.broadcasted_iota(jnp.int32, shape, 1) * 2 + zl) * 128 + lax.broadcasted_iota(jnp.int32, shape, 2)
    weighted = factor * parts + jnp.where(j_ids == i_ids, slope_j[:, None, None], 0.0)
    weighted = weighted.reshape(32, 512)

    weighted = jnp.concatenate([weighted, shifted(weighted, "zl", 1)], axis=1)
    weighted = ring_parts(weighted, "y").reshape(128, 1024)
    z = lax.dot_general(
        weighted, picked, (((1,), (1,)), ((), ())),
        precision=lax.Precision.HIGH, preferred_element_type=jnp.float32,
    )
    z = ring_parts(z, "x")
    cores = jnp.stack([z, shifted(z, "c", 1)])
    cores = jnp.where(c == 0, cores, cores[::-1])
    ordered = jnp.stack(
        [lax.dynamic_index_in_dim(cores, slot_of(((q ^ (2 * zl)) - x) % 4), 1, keepdims=False) for q in range(4)]
    )
    ordered = ordered.reshape(2, 2, 2, 4, 32, -1).transpose(5, 0, 3, 1, 2, 4).reshape(-1, 1024)
    blocks = [
        [mode_vectors], [below], [above], far,
        [other_a, other_b, other_c],
        [other_below_a, other_below_b, other_below_c],
        [other_above_a, other_above_b, other_above_c],
        [*other_far, other_far_c],
    ]
    return slab_part(ordered, blocks)


def solution(mesh):
    torus = Mesh(mesh.devices.reshape(4, 2, 2, 4, 2), ("x", "zh", "c", "y", "zl"))
    return jax.shard_map(
        local,
        mesh=torus,
        in_specs=(P(HARM, MODE), P(HARM, MODE), P(HARM, MODE), P(), P(), P()),
        out_specs=P(MODE, HARM),
        check_vma=False,
    )
```

```python
import jax
import jax.numpy as jnp
from jax import lax
from jax.experimental import pallas as pl
from jax.experimental.pallas import tpu as pltpu
from jax.sharding import Mesh
from jax.sharding import PartitionSpec as P

HARM = ("x", "zh", "c")
MODE = ("y", "zl")
SIZES = {"x": 4, "zh": 2, "c": 2, "y": 4, "zl": 2, ("zh", "zl"): 4}
regular = 0.01
TILE = 384
VMEM = 60 * 1024 * 1024


def shifted(array, axis, step):
    n = SIZES[axis]
    return lax.ppermute(array, axis, [(i, (i + step) % n) for i in range(n)])


def pick(parts, number):
    return lax.dynamic_index_in_dim(parts, number, 0, keepdims=False)


def slot_of(offset):
    return jnp.where(offset == 0, 0, jnp.where(offset == 3, 1, jnp.where(offset == 1, 2, 3)))


def ring_parts(array, axis):
    return [array, shifted(array, axis, 1), shifted(array, axis, -1), shifted(array, axis, 2)]


def split(value):
    high = value.astype(jnp.bfloat16)
    low = (value - high.astype(jnp.float32)).astype(jnp.bfloat16)
    return high, low


def three_pass(a, b, dims):
    a_high, a_low = a
    b_high, b_low = b
    def dot(p, q):
        return lax.dot_general(p, q, (dims, ((), ())), preferred_element_type=jnp.float32)
    return dot(a_high, b_high) + dot(a_high, b_low) + dot(a_low, b_high)


SMALL = pl.CostEstimate(flops=1000, bytes_accessed=1000, transcendentals=0)
ANY = pl.BlockSpec(memory_space=pl.ANY)
STEP = 384
PARAMS = pltpu.CompilerParams(vmem_limit_bytes=VMEM)


def rows_of(array, first, count, after=()):
    step = 3 * STEP
    start = first // step

    def body(source, *refs):
        refs[-1][...] = source[...]

    return pl.pallas_call(
        body,
        grid=(count // step,),
        in_specs=[pl.BlockSpec((step, 128), lambda i: (start + i, 0))] + [ANY] * len(after),
        out_specs=pl.BlockSpec((step, 128), lambda i: (i, 0)),
        out_shape=jax.ShapeDtypeStruct((count, 128), array.dtype),
        compiler_params=PARAMS,
        cost_estimate=SMALL,
    )(array, *after)


def held(array, after):
    def body(source, *refs):
        refs[-1][...] = source[...]

    return pl.pallas_call(
        body,
        in_specs=[pl.BlockSpec(memory_space=pltpu.VMEM)] + [ANY] * len(after),
        out_specs=pl.BlockSpec(memory_space=pltpu.VMEM),
        out_shape=jax.ShapeDtypeStruct(array.shape, array.dtype),
        cost_estimate=SMALL,
    )(array, *after)


def released(array, after):
    def body(*refs):
        pass

    return pl.pallas_call(
        body,
        in_specs=[ANY] * (1 + len(after)),
        out_specs=ANY,
        out_shape=jax.ShapeDtypeStruct(array.shape, array.dtype),
        input_output_aliases={0: 0},
        cost_estimate=SMALL,
    )(array, *after)


def x_parts(kept, came):
    def body(kept_ref, came_ref, *refs):
        x = lax.axis_index("x")
        for ref, offset in zip(refs[-4:], (0, 1, 3, 2), strict=True):
            share = lax.rem(x + offset, 4)
            ref[...] = kept_ref[share] + came_ref[share]

    return pl.pallas_call(
        body,
        in_specs=[pl.BlockSpec(kept.shape, lambda: (0, 0, 0))] * 2,
        out_shape=[jax.ShapeDtypeStruct(kept.shape[1:], kept.dtype)] * 4,
        compiler_params=PARAMS,
        cost_estimate=SMALL,
    )(kept, came)


def cot_ready(own, other):
    rows = own.shape[0]

    def body(own_ref, other_ref, high, low):
        high[...], low[...] = split(jnp.concatenate([own_ref[...].T, other_ref[...].T], axis=0))

    shape = jax.ShapeDtypeStruct((256, rows), jnp.bfloat16)
    return pl.pallas_call(
        body,
        grid=(rows // STEP,),
        in_specs=[pl.BlockSpec((STEP, 128), lambda i: (i, 0))] * 2,
        out_specs=[pl.BlockSpec((256, STEP), lambda i: (0, i))] * 2,
        out_shape=[shape, shape],
        compiler_params=PARAMS,
        cost_estimate=SMALL,
    )(own, other)


def wide(ref):
    return jnp.concatenate([ref[k] for k in range(4)], axis=1)


def gram_shares(cot, whole_x, cut, after):
    rows = whole_x.shape[1]
    steps, start = rows // STEP, cut // STEP

    def body(cot_high, cot_low, x_ref, *refs):
        kept, sent, tail, total = refs[-4:]
        step = pl.program_id(0)
        c, zl = lax.axis_index("c"), lax.axis_index("zl")

        @pl.when(step == 0)
        def _():
            total[...] = jnp.zeros_like(total)

        total[...] += three_pass((cot_high[...], cot_low[...]), split(wide(x_ref)), ((1,), (0,)))

        @pl.when(step >= start)
        def _():
            tail[...] = x_ref[...]

        @pl.when(step == steps - 1)
        def _():
            for s in range(4):
                for ref, core in ((kept, c), (sent, 1 - c)):
                    row = pl.multiple_of(lax.rem(s * 64 + core * 32 + 128 * zl, 256), 32)
                    ref[s] = total[pl.ds(row, 32), :]

    shape = jax.ShapeDtypeStruct((4, 32, 512), jnp.float32)
    whole = pl.BlockSpec((4, 32, 512), lambda i: (0, 0, 0))
    return pl.pallas_call(
        body,
        grid=(steps,),
        in_specs=[pl.BlockSpec((256, STEP), lambda i: (0, i))] * 2
        + [pl.BlockSpec((4, STEP, 128), lambda i: (0, i, 0))]
        + [ANY] * len(after),
        out_specs=[whole, whole, pl.BlockSpec((4, STEP, 128), lambda i: (0, jnp.maximum(i - start, 0), 0))],
        out_shape=[shape, shape, jax.ShapeDtypeStruct((4, rows - cut, 128), jnp.float32)],
        scratch_shapes=[pltpu.VMEM((256, 512), jnp.float32)],
        compiler_params=PARAMS,
        cost_estimate=SMALL,
    )(*cot, whole_x, *after)


def z_part(weighted, own, other):
    share, depth = own[0].shape

    def body(*refs):
        weighted_refs, own_refs, other_refs = refs[:4], refs[4:8], refs[8:12]
        out, tall, rows = refs[-3:]
        x, c, y = lax.axis_index("x"), lax.axis_index("c"), lax.axis_index("y")
        for slot, offset in enumerate((0, 3, 1, 2)):
            tall[pl.ds(pl.multiple_of(lax.rem(y + offset, 4) * 32, 32), 32), :] = weighted_refs[slot][...]
            source = lax.rem(x + offset, 4)
            for which, value in ((c, own_refs[slot][...]), (1 - c, other_refs[slot][...])):
                rows[pl.ds(pl.multiple_of((source * 2 + which) * share, share), share), :] = value
        out[...] = three_pass(split(tall[...]), split(rows[...]), ((1,), (1,)))

    return pl.pallas_call(
        body,
        out_shape=jax.ShapeDtypeStruct((128, 8 * share), jnp.float32),
        scratch_shapes=[pltpu.VMEM((128, depth), jnp.float32), pltpu.VMEM((8 * share, depth), jnp.float32)],
        compiler_params=PARAMS,
        cost_estimate=SMALL,
    )(*weighted, *own, *other)


def z_ready(own_z, other_z):
    depth, height = 1024, own_z[0].shape[1]

    def body(*refs):
        sets, (z_high, z_low, z_tall) = (refs[:4], refs[4:8]), refs[8:]
        x, c, zl = lax.axis_index("x"), lax.axis_index("c"), lax.axis_index("zl")
        for slot, offset in enumerate((0, 3, 1, 2)):
            source = lax.rem(x + offset, 4)
            side = lax.rem(source // 2 + zl, 2)
            for part in range(4):
                for which, held in ((c, sets[0]), (1 - c, sets[1])):
                    row = side * 512 + part * 128 + lax.rem(source, 2) * 64 + which * 32
                    z_tall[pl.ds(pl.multiple_of(row, 32), 32), :] = held[slot][part * 32 : part * 32 + 32, :]
        for part in range(depth // 128):
            cols = slice(part * 128, part * 128 + 128)
            z_high[:, cols], z_low[:, cols] = split(z_tall[cols, :].T)

    shape = jax.ShapeDtypeStruct((height, depth), jnp.bfloat16)
    return pl.pallas_call(
        body,
        out_shape=[shape, shape],
        scratch_shapes=[pltpu.VMEM((depth, height), jnp.float32)],
        compiler_params=PARAMS,
        cost_estimate=SMALL,
    )(*own_z, *other_z)


def slab_part(z, own_x, own_first, other_x, slab, first, count, total):
    steps = count // STEP
    own_start, start = own_first // STEP, first // STEP
    height, depth = z[0].shape

    def body(z_high, z_low, own_ref, other_ref, *refs):
        x_tile = split(jnp.concatenate([wide(own_ref), wide(other_ref)], axis=1))
        refs[-1][...] = three_pass((z_high[...], z_low[...]), x_tile, ((1,), (1,)))

    return pl.pallas_call(
        body,
        grid=(steps,),
        in_specs=[pl.BlockSpec((height, depth), lambda i: (0, 0))] * 2
        + [
            pl.BlockSpec((4, STEP, 128), lambda i: (0, own_start + i, 0)),
            pl.BlockSpec((4, STEP, 128), lambda i: (0, i, 0)),
        ]
        + ([] if slab is None else [ANY]),
        out_specs=pl.BlockSpec((height, STEP), lambda i: (0, start + i)),
        out_shape=jax.ShapeDtypeStruct((height, total), jnp.float32),
        input_output_aliases={} if slab is None else {4: 0},
        compiler_params=PARAMS,
        cost_estimate=SMALL,
    )(*z, own_x, other_x, *([] if slab is None else [slab]))


def places(slab_rows, height, count):
    total = slab_rows.shape[0]
    kinds = total // count
    block_of = slab_rows // height
    member = (block_of[:, None] == jnp.arange(kinds)[None, :]).astype(jnp.float32).reshape(-1, 128, kinds)
    before = jnp.tril(jnp.ones((128, 128), jnp.float32), -1)
    within = jnp.einsum("ab,cbh->cah", before, member, preferred_element_type=jnp.float32)
    chunks = member.shape[0]
    sums = member.sum(1)
    ahead = jnp.dot(jnp.tril(jnp.ones((chunks, chunks), jnp.float32), -1), sums, preferred_element_type=jnp.float32)
    rank = ((within + ahead[:, None, :]) * member).sum(2).reshape(total)
    return block_of * count + rank.astype(jnp.int32)


def slab_weights(weights, slab_rows, x, zh, c):
    height = weights.shape[0]
    total = slab_rows.shape[0]
    count = total // 16
    harm = (x * 2 + zh) * 2 + c
    place = places(slab_rows, height, count)
    ids = harm * count + jnp.arange(count, dtype=jnp.int32)
    own = jnp.where(place[None, :] == ids[:, None], slab_rows[None, :] - harm * height, 0).sum(1)
    rows = jnp.take(weights, own, axis=0, mode="clip")
    pair = jnp.stack([rows, shifted(rows, "zh", 1)])
    ring = jnp.stack(ring_parts(pair, "x"))
    every = jnp.stack([ring, shifted(ring, "c", 1)])
    every = every.reshape(-1, 128)
    share = total // 8 // 8
    wanted = lax.dynamic_slice_in_dim(place.reshape(8, 8, share), x * 2 + c, 1, axis=1).reshape(-1)
    source, row = wanted // count, wanted % count
    source_x, source_zh, source_c = source // 4, (source // 2) % 2, source % 2
    held = (
        ((source_c != c) * 4 + slot_of((source_x - x) % 4)) * 2 + (source_zh != zh)
    ) * count + row
    return jnp.take(every, held, axis=0, mode="clip").reshape(8, share, 128)


def slab_share(chosen, zl):
    share = chosen.shape[1]
    came = lax.all_to_all(chosen, MODE, 0, 0, tiled=True).reshape(4, 2, share, 128)
    came = jnp.where(zl == 0, came, came[:, ::-1])
    return came.transpose(2, 1, 0, 3).reshape(share, 1024)


def local(mode_vectors, weights, cotangent, eigenvalues, eigen_cotangent, slab_rows):
    x, zh, c, y, zl = (lax.axis_index(a) for a in ("x", "zh", "c", "y", "zl"))
    rows = mode_vectors.shape[0]
    cut = rows * 3 // 4
    own_x = lax.all_gather(mode_vectors, "y")
    other_cot = shifted(cotangent, "zl", 1)
    chosen = slab_weights(weights, slab_rows, x, zh, c)
    share = slab_share(held(chosen, (other_cot,)), zl)
    other_rows = shifted(rows_of(mode_vectors, 0, cut, (other_cot, share)), "zl", 1)
    own_share = ring_parts(share, "x")
    other_share = [shifted(part, "c", 1) for part in own_share]
    cot = cot_ready(cotangent, other_cot)

    kept, sent, tail = gram_shares(cot, own_x, cut, own_share)
    other_low = lax.all_gather(rows_of(other_rows, 0, cut, (kept,)), "y")
    to_self, to_above, to_below, to_far = x_parts(kept, shifted(sent, "c", 1))
    total = to_self + shifted(to_above, "x", 1) + shifted(to_below, "x", -1) + shifted(to_far, "x", 2)
    own, below, above, far = ring_parts(total, ("zh", "zl"))
    total = jnp.concatenate([own + far, below + above], axis=1)
    j_first = (y * 2 + x // 2) * 128 + ((x % 2) * 2 + c) * 32
    eigen_j = lax.dynamic_slice_in_dim(eigenvalues, j_first, 32)
    slope_j = lax.dynamic_slice_in_dim(eigen_cotangent, j_first, 32)
    sides = eigenvalues.reshape(4, 2, 128).transpose(1, 0, 2).reshape(2, 512)
    eigen_i = jnp.where(zl == 0, sides, sides[::-1]).reshape(1024)
    differ = eigen_j[:, None] - eigen_i[None]
    factor = differ / (differ * differ + regular)
    j_ids = j_first + lax.broadcasted_iota(jnp.int32, (32, 1024), 0)
    col = lax.broadcasted_iota(jnp.int32, (32, 1024), 1)
    i_ids = (col % 512 // 128 * 2 + (zl + col // 512) % 2) * 128 + col % 128
    weighted = factor * total + jnp.where(j_ids == i_ids, slope_j[:, None], 0.0)

    other_high = shifted(released(tail, (weighted,)), "zl", 1)
    z_own = ring_parts(z_part(ring_parts(weighted, "y"), own_share, other_share), "x")
    z_other = [shifted(part, "c", 1) for part in z_own]
    z = z_ready(z_own, z_other)
    slab = slab_part(z, own_x, 0, other_low, None, 0, cut, rows)
    return slab_part(z, own_x, cut, other_high, slab, cut, rows - cut, rows)


def solution(mesh):
    torus = Mesh(mesh.devices.reshape(4, 2, 2, 4, 2), ("x", "zh", "c", "y", "zl"))
    return jax.shard_map(
        local,
        mesh=torus,
        in_specs=(P(HARM, MODE), P(HARM, MODE), P(HARM, MODE), P(), P(), P()),
        out_specs=P(MODE, HARM),
        check_vma=False,
    )
```

```python
import jax
import jax.numpy as jnp
from jax import lax
from jax.experimental import pallas as pl
from jax.experimental.pallas import tpu as pltpu
from jax.sharding import Mesh
from jax.sharding import PartitionSpec as P

HARM = ("x", "zh", "c")
MODE = ("y", "zl")
SIZES = {"x": 4, "zh": 2, "c": 2, "y": 4, "zl": 2, ("zh", "zl"): 4}
regular = 0.01
TILE = 384
VMEM = 60 * 1024 * 1024


def shifted(array, axis, step):
    n = SIZES[axis]
    return lax.ppermute(array, axis, [(i, (i + step) % n) for i in range(n)])


def pick(parts, number):
    return lax.dynamic_index_in_dim(parts, number, 0, keepdims=False)


def slot_of(offset):
    return jnp.where(offset == 0, 0, jnp.where(offset == 3, 1, jnp.where(offset == 1, 2, 3)))


def ring_parts(array, axis):
    return [array, shifted(array, axis, 1), shifted(array, axis, -1), shifted(array, axis, 2)]


def split(value):
    high = value.astype(jnp.bfloat16)
    low = (value - high.astype(jnp.float32)).astype(jnp.bfloat16)
    return high, low


def three_pass(both, b, dims):
    high, low = b
    rows = both.shape[0] // 2

    def dot(p, q):
        return lax.dot_general(p, q, (dims, ((), ())), preferred_element_type=jnp.float32)

    first = dot(both, high)
    return first[:rows] + first[rows:] + dot(both[:rows], low)


SMALL = pl.CostEstimate(flops=1000, bytes_accessed=1000, transcendentals=0)
ANY = pl.BlockSpec(memory_space=pl.ANY)
STEP = 384
WIDE = 768
PARAMS = pltpu.CompilerParams(vmem_limit_bytes=VMEM)


def with_rows(small, array, count, after):
    rows = count // 2

    def body(array_ref, small_ref, *refs):
        refs[-1][...] = array_ref[...]

    return pl.pallas_call(
        body,
        grid=(2,),
        in_specs=[pl.BlockSpec((rows, 128), lambda i: (i, 0)), ANY] + [ANY] * len(after),
        out_specs=[ANY, pl.BlockSpec((rows, 128), lambda i: (i, 0))],
        out_shape=[
            jax.ShapeDtypeStruct(small.shape, small.dtype),
            jax.ShapeDtypeStruct((count, 128), array.dtype),
        ],
        input_output_aliases={1: 0},
        compiler_params=PARAMS,
        cost_estimate=SMALL,
    )(array, small, *after)


def released(array, after):
    def body(*refs):
        pass

    return pl.pallas_call(
        body,
        in_specs=[ANY] * (1 + len(after)),
        out_specs=ANY,
        out_shape=jax.ShapeDtypeStruct(array.shape, array.dtype),
        input_output_aliases={0: 0},
        cost_estimate=SMALL,
    )(array, *after)


def x_parts(kept, came, after):
    def body(kept_ref, came_ref, *refs):
        x = lax.axis_index("x")
        for ref, offset in zip(refs[-4:], (0, 1, 3, 2), strict=True):
            share = lax.rem(x + offset, 4)
            ref[...] = kept_ref[share] + came_ref[share]

    return pl.pallas_call(
        body,
        in_specs=[pl.BlockSpec(kept.shape, lambda: (0, 0, 0))] * 2 + [ANY] * len(after),
        out_shape=[jax.ShapeDtypeStruct(kept.shape[1:], kept.dtype)] * 4,
        compiler_params=PARAMS,
        cost_estimate=SMALL,
    )(kept, came, *after)


def cot_ready(own, first, second):
    rows = own.shape[0]
    split_at = first.shape[0] // STEP

    def body(own_ref, first_ref, second_ref, both):
        other = jnp.where(pl.program_id(0) < split_at, first_ref[...], second_ref[...])
        high, low = split(jnp.concatenate([own_ref[...].T, other.T], axis=0))
        both[:256], both[256:] = high, low

    return pl.pallas_call(
        body,
        grid=(rows // STEP,),
        in_specs=[
            pl.BlockSpec((STEP, 128), lambda i: (i, 0)),
            pl.BlockSpec((STEP, 128), lambda i: (jnp.minimum(i, split_at - 1), 0)),
            pl.BlockSpec((STEP, 128), lambda i: (jnp.maximum(i - split_at, 0), 0)),
        ],
        out_specs=pl.BlockSpec((512, STEP), lambda i: (0, i)),
        out_shape=jax.ShapeDtypeStruct((512, rows), jnp.bfloat16),
        compiler_params=PARAMS,
        cost_estimate=SMALL,
    )(own, first, second)


def wide(ref):
    return jnp.concatenate([ref[k] for k in range(4)], axis=1)


def gram_shares(cot, whole_x, cut, after):
    rows = whole_x.shape[1]
    step_rows = rows - cut
    steps, start = rows // step_rows, cut // step_rows

    def body(cot_ref, x_ref, *refs):
        kept, sent, tail, total = refs[-4:]
        step = pl.program_id(0)
        c, zl = lax.axis_index("c"), lax.axis_index("zl")

        @pl.when(step == 0)
        def _():
            total[...] = jnp.zeros_like(total)

        total[...] += three_pass(cot_ref[...], split(wide(x_ref)), ((1,), (0,)))

        @pl.when(step >= start)
        def _():
            tail[...] = x_ref[...]

        @pl.when(step == steps - 1)
        def _():
            for s in range(4):
                for ref, core in ((kept, c), (sent, 1 - c)):
                    row = pl.multiple_of(lax.rem(s * 64 + core * 32 + 128 * zl, 256), 32)
                    ref[s] = total[pl.ds(row, 32), :]

    shape = jax.ShapeDtypeStruct((4, 32, 512), jnp.float32)
    whole = pl.BlockSpec((4, 32, 512), lambda i: (0, 0, 0))
    return pl.pallas_call(
        body,
        grid=(steps,),
        in_specs=[pl.BlockSpec((512, step_rows), lambda i: (0, i))]
        + [pl.BlockSpec((4, step_rows, 128), lambda i: (0, i, 0))]
        + [ANY] * len(after),
        out_specs=[whole, whole, pl.BlockSpec((4, step_rows, 128), lambda i: (0, 0, 0))],
        out_shape=[shape, shape, jax.ShapeDtypeStruct((4, rows - cut, 128), jnp.float32)],
        scratch_shapes=[pltpu.VMEM((256, 512), jnp.float32)],
        compiler_params=PARAMS,
        cost_estimate=SMALL,
    )(cot, whole_x, *after)


def z_part(weighted, picked):
    height, depth = picked.shape

    def body(*refs):
        weighted_refs, picked_ref = refs[:4], refs[4]
        out, tall = refs[-2:]
        y = lax.axis_index("y")
        for slot, offset in enumerate((0, 3, 1, 2)):
            tall[pl.ds(pl.multiple_of(lax.rem(y + offset, 4) * 32, 32), 32), :] = weighted_refs[slot][...]
        out[...] = three_pass(jnp.concatenate(split(tall[...]), axis=0), split(picked_ref[...]), ((1,), (1,)))

    return pl.pallas_call(
        body,
        out_shape=jax.ShapeDtypeStruct((128, height), jnp.float32),
        scratch_shapes=[pltpu.VMEM((128, depth), jnp.float32)],
        compiler_params=PARAMS,
        cost_estimate=SMALL,
    )(*weighted, picked)


def z_ready(own_z, other_z):
    depth, height = 1024, own_z[0].shape[1]

    def body(*refs):
        sets, (both, z_tall) = (refs[:4], refs[4:8]), refs[8:]
        x, c, zl = lax.axis_index("x"), lax.axis_index("c"), lax.axis_index("zl")
        for slot, offset in enumerate((0, 3, 1, 2)):
            source = lax.rem(x + offset, 4)
            side = lax.rem(source // 2 + zl, 2)
            for part in range(4):
                for which, held in ((c, sets[0]), (1 - c, sets[1])):
                    row = side * 512 + part * 128 + lax.rem(source, 2) * 64 + which * 32
                    z_tall[pl.ds(pl.multiple_of(row, 32), 32), :] = held[slot][part * 32 : part * 32 + 32, :]
        for part in range(depth // 128):
            cols = slice(part * 128, part * 128 + 128)
            both[:height, cols], both[height:, cols] = split(z_tall[cols, :].T)

    return pl.pallas_call(
        body,
        out_shape=jax.ShapeDtypeStruct((2 * height, depth), jnp.bfloat16),
        scratch_shapes=[pltpu.VMEM((depth, height), jnp.float32)],
        compiler_params=PARAMS,
        cost_estimate=SMALL,
    )(*own_z, *other_z)


def slab_part(z, own_x, other_low, other_high):
    total = own_x.shape[1]
    split_at = other_low.shape[1] // WIDE
    height, depth = z.shape[0] // 2, z.shape[1]

    def body(z_ref, own_ref, low_ref, high_ref, out):
        step = pl.program_id(0)

        def product(other_ref):
            x_tile = split(jnp.concatenate([wide(own_ref), wide(other_ref)], axis=1))
            out[...] = three_pass(z_ref[...], x_tile, ((1,), (1,)))

        @pl.when(step < split_at)
        def _():
            product(low_ref)

        @pl.when(step >= split_at)
        def _():
            product(high_ref)

    return pl.pallas_call(
        body,
        grid=(total // WIDE,),
        in_specs=[
            pl.BlockSpec(z.shape, lambda i: (0, 0)),
            pl.BlockSpec((4, WIDE, 128), lambda i: (0, i, 0)),
            pl.BlockSpec((4, WIDE, 128), lambda i: (0, jnp.minimum(i, split_at - 1), 0)),
            pl.BlockSpec((4, WIDE, 128), lambda i: (0, jnp.maximum(i - split_at, 0), 0)),
        ],
        out_specs=pl.BlockSpec((height, WIDE), lambda i: (0, i)),
        out_shape=jax.ShapeDtypeStruct((height, total), jnp.float32),
        compiler_params=PARAMS,
        cost_estimate=SMALL,
    )(z, own_x, other_low, other_high)


def places(slab_rows, height, count):
    total = slab_rows.shape[0]
    kinds = total // count
    block_of = slab_rows // height
    member = (block_of[:, None] == jnp.arange(kinds)[None, :]).astype(jnp.float32).reshape(-1, 128, kinds)
    before = jnp.tril(jnp.ones((128, 128), jnp.float32), -1)
    within = jnp.einsum("ab,cbh->cah", before, member, preferred_element_type=jnp.float32)
    chunks = member.shape[0]
    sums = member.sum(1)
    ahead = jnp.dot(jnp.tril(jnp.ones((chunks, chunks), jnp.float32), -1), sums, preferred_element_type=jnp.float32)
    rank = ((within + ahead[:, None, :]) * member).sum(2).reshape(total)
    return block_of * count + rank.astype(jnp.int32)


def slab_weights(weights, slab_rows, x, zh, c, zl, cots, mode_vectors, cut):
    height = weights.shape[0]
    total = slab_rows.shape[0]
    count = total // 16
    harm = (x * 2 + zh) * 2 + c
    place = places(slab_rows, height, count)
    ids = harm * count + jnp.arange(count, dtype=jnp.int32)
    local_rows = jnp.where(place[None, :] == ids[:, None], slab_rows[None, :] - harm * height, 0).sum(1)
    own, below, above, far = ring_parts(jnp.take(weights, local_rows, axis=0, mode="clip"), ("zh", "zl"))
    near = jnp.concatenate([own, jnp.where(zl == 0, above, below)], axis=1)
    away = jnp.concatenate([far, jnp.where(zl == 0, below, above)], axis=1)
    pair, first_rows = with_rows(jnp.stack([near, away]), mode_vectors, cut, cots[:1])
    ring = jnp.stack(ring_parts(pair, "x")).reshape(-1, 256)
    share = total // 64
    places_here = pick(place.reshape(4, 2, 4, 2, share).swapaxes(0, 1), zl)
    places_here = lax.dynamic_index_in_dim(places_here, x, 1, keepdims=False)

    def chosen(core):
        wanted = lax.dynamic_index_in_dim(places_here, core, 1, keepdims=False).reshape(-1)
        source, row = wanted // count, wanted % count
        source_x, source_zh, source_c = source // 4, (source // 2) % 2, source % 2
        number = (slot_of((source_x - x) % 4) * 2 + (source_zh != zh)) * count + row
        return number, source_c == c

    numbers, mine = zip(chosen(c), chosen(1 - c), strict=True)
    taken = jnp.take(ring, jnp.concatenate(numbers), axis=0, mode="clip")
    taken = jnp.where(jnp.concatenate(mine)[:, None], taken, 0.0).reshape(2, 4, share, 256)
    taken = released(taken, cots[1:])
    return taken[0] + shifted(taken[1], "c", 1), first_rows


def slab_share(chosen, y):
    share = chosen.shape[1]
    came = jnp.stack(
        [
            pick(chosen, y),
            shifted(pick(chosen, (y + 1) % 4), "y", 1),
            shifted(pick(chosen, (y + 3) % 4), "y", -1),
            shifted(pick(chosen, (y + 2) % 4), "y", 2),
        ]
    )
    came = jnp.stack([pick(came, slot_of((k - y) % 4)) for k in range(4)])
    return came.reshape(4, share, 2, 128).transpose(1, 2, 0, 3).reshape(share, 1024)


def local(mode_vectors, weights, cotangent, eigenvalues, eigen_cotangent, slab_rows):
    x, zh, c, y, zl = (lax.axis_index(a) for a in ("x", "zh", "c", "y", "zl"))
    rows = mode_vectors.shape[0]
    cut = rows * 3 // 4
    own_x = lax.all_gather(mode_vectors, "y")
    early = rows // 4
    cots = (shifted(cotangent[:early], "zl", 1), shifted(cotangent[early:], "zl", 1))
    chosen, first_rows = slab_weights(weights, slab_rows, x, zh, c, zl, cots, mode_vectors, cut)
    other_rows = shifted(released(first_rows, cots), "zl", 1)
    share = slab_share(chosen, y)
    picked = lax.all_gather(share, ("x", "c"), tiled=True)
    cot = cot_ready(cotangent, *cots)

    kept, sent, tail = gram_shares(cot, own_x, cut, (share,))
    to_self, to_above, to_below, to_far = x_parts(kept, shifted(sent, "c", 1), ())
    other_low = lax.all_gather(released(other_rows, (to_self,)), "y")
    total = to_self + shifted(to_above, "x", 1) + shifted(to_below, "x", -1) + shifted(to_far, "x", 2)
    own, below, above, far = ring_parts(total, ("zh", "zl"))
    total = jnp.concatenate([own + far, below + above], axis=1)
    j_first = (y * 2 + x // 2) * 128 + ((x % 2) * 2 + c) * 32
    eigen_j = lax.dynamic_slice_in_dim(eigenvalues, j_first, 32)
    slope_j = lax.dynamic_slice_in_dim(eigen_cotangent, j_first, 32)
    sides = eigenvalues.reshape(4, 2, 128).transpose(1, 0, 2).reshape(2, 512)
    eigen_i = jnp.where(zl == 0, sides, sides[::-1]).reshape(1024)
    differ = eigen_j[:, None] - eigen_i[None]
    factor = differ / (differ * differ + regular)
    j_ids = j_first + lax.broadcasted_iota(jnp.int32, (32, 1024), 0)
    col = lax.broadcasted_iota(jnp.int32, (32, 1024), 1)
    i_ids = (col % 512 // 128 * 2 + (zl + col // 512) % 2) * 128 + col % 128
    weighted = factor * total + jnp.where(j_ids == i_ids, slope_j[:, None], 0.0)

    other_high = shifted(released(tail, (weighted,)), "zl", 1)
    z_own = ring_parts(z_part(ring_parts(weighted, "y"), picked), "x")
    z_other = [shifted(part, "c", 1) for part in z_own]
    z = z_ready(z_own, z_other)
    return slab_part(z, own_x, other_low, other_high)


def solution(mesh):
    torus = Mesh(mesh.devices.reshape(4, 2, 2, 4, 2), ("x", "zh", "c", "y", "zl"))
    return jax.shard_map(
        local,
        mesh=torus,
        in_specs=(P(HARM, MODE), P(HARM, MODE), P(HARM, MODE), P(), P(), P()),
        out_specs=P(MODE, HARM),
        check_vma=False,
    )
```

```python
import jax
import jax.numpy as jnp
from jax import lax
from jax.experimental import pallas as pl
from jax.experimental.pallas import tpu as pltpu
from jax.sharding import Mesh
from jax.sharding import PartitionSpec as P

HARM = ("x", "zh", "c")
MODE = ("y", "zl")
SIZES = {"x": 4, "zh": 2, "c": 2, "y": 4, "zl": 2, ("zh", "zl"): 4}
regular = 0.01
TILE = 384
VMEM = 60 * 1024 * 1024


def shifted(array, axis, step):
    n = SIZES[axis]
    return lax.ppermute(array, axis, [(i, (i + step) % n) for i in range(n)])


def pick(parts, number):
    return lax.dynamic_index_in_dim(parts, number, 0, keepdims=False)


def slot_of(offset):
    return jnp.where(offset == 0, 0, jnp.where(offset == 3, 1, jnp.where(offset == 1, 2, 3)))


def ring_parts(array, axis):
    return [array, shifted(array, axis, 1), shifted(array, axis, -1), shifted(array, axis, 2)]


def split(value):
    high = value.astype(jnp.bfloat16)
    low = (value - high.astype(jnp.float32)).astype(jnp.bfloat16)
    return high, low


def three_pass(both, b, dims):
    high, low = b
    rows = both.shape[0] // 2

    def dot(p, q):
        return lax.dot_general(p, q, (dims, ((), ())), preferred_element_type=jnp.float32)

    first = dot(both, high)
    return first[:rows] + first[rows:] + dot(both[:rows], low)


SMALL = pl.CostEstimate(flops=1000, bytes_accessed=1000, transcendentals=0)
ANY = pl.BlockSpec(memory_space=pl.ANY)
STEP = 384
WIDE = 768
PARAMS = pltpu.CompilerParams(vmem_limit_bytes=VMEM)


def with_pieces(small, array, cut, after):
    rows = cut // 2

    def body(array_ref, small_ref, *refs):
        first, second = refs[-2:]
        step = pl.program_id(0)

        @pl.when(step == 0)
        def _():
            first[...] = array_ref[...]

        @pl.when(step == 1)
        def _():
            second[...] = array_ref[...]

    piece = jax.ShapeDtypeStruct((rows, 128), array.dtype)
    return pl.pallas_call(
        body,
        grid=(2,),
        in_specs=[pl.BlockSpec((rows, 128), lambda i: (i, 0)), ANY] + [ANY] * len(after),
        out_specs=[ANY] + [pl.BlockSpec((rows, 128), lambda i: (0, 0))] * 2,
        out_shape=[jax.ShapeDtypeStruct(small.shape, small.dtype), piece, piece],
        input_output_aliases={1: 0},
        compiler_params=PARAMS,
        cost_estimate=SMALL,
    )(array, small, *after)


def released(array, after):
    def body(*refs):
        pass

    return pl.pallas_call(
        body,
        in_specs=[ANY] * (1 + len(after)),
        out_specs=ANY,
        out_shape=jax.ShapeDtypeStruct(array.shape, array.dtype),
        input_output_aliases={0: 0},
        cost_estimate=SMALL,
    )(array, *after)


def x_parts(kept, came, after):
    def body(kept_ref, came_ref, *refs):
        x = lax.axis_index("x")
        for ref, offset in zip(refs[-4:], (0, 1, 3, 2), strict=True):
            share = lax.rem(x + offset, 4)
            ref[...] = kept_ref[share] + came_ref[share]

    return pl.pallas_call(
        body,
        in_specs=[pl.BlockSpec(kept.shape, lambda: (0, 0, 0))] * 2 + [ANY] * len(after),
        out_shape=[jax.ShapeDtypeStruct(kept.shape[1:], kept.dtype)] * 4,
        compiler_params=PARAMS,
        cost_estimate=SMALL,
    )(kept, came, *after)


def joined(first, second, after):
    rows = first.shape[0]

    def body(first_ref, second_ref, *refs):
        @pl.when(pl.program_id(0) == 0)
        def _():
            refs[-1][...] = first_ref[...]

        @pl.when(pl.program_id(0) == 1)
        def _():
            refs[-1][...] = second_ref[...]

    return pl.pallas_call(
        body,
        grid=(2,),
        in_specs=[pl.BlockSpec((rows, 128), lambda i: (0, 0))] * 2 + [ANY] * len(after),
        out_specs=pl.BlockSpec((rows, 128), lambda i: (i, 0)),
        out_shape=jax.ShapeDtypeStruct((2 * rows, 128), first.dtype),
        compiler_params=PARAMS,
        cost_estimate=SMALL,
    )(first, second, *after)


def cot_ready(own, first, second):
    rows = own.shape[0]
    split_at = first.shape[0] // STEP

    def body(own_ref, first_ref, second_ref, both):
        other = jnp.where(pl.program_id(0) < split_at, first_ref[...], second_ref[...])
        high, low = split(jnp.concatenate([own_ref[...].T, other.T], axis=0))
        both[:256], both[256:] = high, low

    return pl.pallas_call(
        body,
        grid=(rows // STEP,),
        in_specs=[
            pl.BlockSpec((STEP, 128), lambda i: (i, 0)),
            pl.BlockSpec((STEP, 128), lambda i: (jnp.minimum(i, split_at - 1), 0)),
            pl.BlockSpec((STEP, 128), lambda i: (jnp.maximum(i - split_at, 0), 0)),
        ],
        out_specs=pl.BlockSpec((512, STEP), lambda i: (0, i)),
        out_shape=jax.ShapeDtypeStruct((512, rows), jnp.bfloat16),
        compiler_params=PARAMS,
        cost_estimate=pl.CostEstimate(flops=1000, bytes_accessed=rows * 4096, transcendentals=0),
    )(own, first, second)


def wide(ref):
    return jnp.concatenate([ref[k] for k in range(4)], axis=1)


def gram_shares(cot, whole_x, cut, after):
    rows = whole_x.shape[1]
    step_rows = rows - cut
    steps, start = rows // step_rows, cut // step_rows

    def body(cot_ref, x_ref, *refs):
        kept, sent, tail, total = refs[-4:]
        step = pl.program_id(0)
        c, zl = lax.axis_index("c"), lax.axis_index("zl")

        @pl.when(step == 0)
        def _():
            total[...] = jnp.zeros_like(total)

        total[...] += three_pass(cot_ref[...], split(wide(x_ref)), ((1,), (0,)))

        @pl.when(step >= start)
        def _():
            tail[...] = x_ref[...]

        @pl.when(step == steps - 1)
        def _():
            for s in range(4):
                for ref, core in ((kept, c), (sent, 1 - c)):
                    row = pl.multiple_of(lax.rem(s * 64 + core * 32 + 128 * zl, 256), 32)
                    ref[s] = total[pl.ds(row, 32), :]

    shape = jax.ShapeDtypeStruct((4, 32, 512), jnp.float32)
    whole = pl.BlockSpec((4, 32, 512), lambda i: (0, 0, 0))
    return pl.pallas_call(
        body,
        grid=(steps,),
        in_specs=[pl.BlockSpec((512, step_rows), lambda i: (0, i))]
        + [pl.BlockSpec((4, step_rows, 128), lambda i: (0, i, 0))]
        + [ANY] * len(after),
        out_specs=[whole, whole, pl.BlockSpec((4, step_rows, 128), lambda i: (0, 0, 0))],
        out_shape=[shape, shape, jax.ShapeDtypeStruct((4, rows - cut, 128), jnp.float32)],
        scratch_shapes=[pltpu.VMEM((256, 512), jnp.float32)],
        compiler_params=PARAMS,
        cost_estimate=SMALL,
    )(cot, whole_x, *after)


def z_part(weighted, own, other):
    count, share, depth = own.shape

    def body(*refs):
        weighted_refs, own_ref, other_ref = refs[:4], refs[4], refs[5]
        out, tall, rows = refs[-3:]
        y, c = lax.axis_index("y"), lax.axis_index("c")
        for slot, offset in enumerate((0, 3, 1, 2)):
            tall[pl.ds(pl.multiple_of(lax.rem(y + offset, 4) * 32, 32), 32), :] = weighted_refs[slot][...]
        for k in range(count):
            for which, ref in ((c, own_ref), (1 - c, other_ref)):
                rows[pl.ds(pl.multiple_of((k * 2 + which) * share, share), share), :] = ref[k]
        out[...] = three_pass(jnp.concatenate(split(tall[...]), axis=0), split(rows[...]), ((1,), (1,)))

    return pl.pallas_call(
        body,
        out_shape=jax.ShapeDtypeStruct((128, 2 * count * share), jnp.float32),
        scratch_shapes=[pltpu.VMEM((128, depth), jnp.float32), pltpu.VMEM((2 * count * share, depth), jnp.float32)],
        compiler_params=PARAMS,
        cost_estimate=SMALL,
    )(*weighted, own, other)


def z_ready(own_z, other_z):
    depth, height = 1024, own_z[0].shape[1]

    def body(*refs):
        sets, (both, z_tall) = (refs[:4], refs[4:8]), refs[8:]
        x, c, zl = lax.axis_index("x"), lax.axis_index("c"), lax.axis_index("zl")
        for slot, offset in enumerate((0, 3, 1, 2)):
            source = lax.rem(x + offset, 4)
            side = lax.rem(source // 2 + zl, 2)
            for part in range(4):
                for which, held in ((c, sets[0]), (1 - c, sets[1])):
                    row = side * 512 + part * 128 + lax.rem(source, 2) * 64 + which * 32
                    z_tall[pl.ds(pl.multiple_of(row, 32), 32), :] = held[slot][part * 32 : part * 32 + 32, :]
        for part in range(depth // 128):
            cols = slice(part * 128, part * 128 + 128)
            both[:height, cols], both[height:, cols] = split(z_tall[cols, :].T)

    return pl.pallas_call(
        body,
        out_shape=jax.ShapeDtypeStruct((2 * height, depth), jnp.bfloat16),
        scratch_shapes=[pltpu.VMEM((depth, height), jnp.float32)],
        compiler_params=PARAMS,
        cost_estimate=SMALL,
    )(*own_z, *other_z)


def slab_own(z, own_x):
    total = own_x.shape[1]
    height, depth = z.shape[0] // 2, z.shape[1] // 2

    def body(z_ref, own_ref, out):
        out[...] = three_pass(z_ref[...], split(wide(own_ref)), ((1,), (1,)))

    return pl.pallas_call(
        body,
        grid=(total // WIDE,),
        in_specs=[
            pl.BlockSpec((2 * height, depth), lambda i: (0, 0)),
            pl.BlockSpec((4, WIDE, 128), lambda i: (0, i, 0)),
        ],
        out_specs=pl.BlockSpec((height, WIDE), lambda i: (0, i)),
        out_shape=jax.ShapeDtypeStruct((height, total), jnp.float32),
        compiler_params=PARAMS,
        cost_estimate=pl.CostEstimate(flops=1000, bytes_accessed=1 << 24, transcendentals=0),
    )(z, own_x)


def slab_other(z, other_low, other_high, slab):
    total = slab.shape[1]
    split_at = other_low.shape[1] // WIDE
    height, depth = z.shape[0] // 2, z.shape[1] // 2

    def body(z_ref, low_ref, high_ref, slab_ref, out):
        step = pl.program_id(0)

        def product(other_ref):
            out[...] = slab_ref[...] + three_pass(z_ref[...], split(wide(other_ref)), ((1,), (1,)))

        @pl.when(step < split_at)
        def _():
            product(low_ref)

        @pl.when(step >= split_at)
        def _():
            product(high_ref)

    tile = pl.BlockSpec((height, WIDE), lambda i: (0, i))
    return pl.pallas_call(
        body,
        grid=(total // WIDE,),
        in_specs=[
            pl.BlockSpec((2 * height, depth), lambda i: (0, 1)),
            pl.BlockSpec((4, WIDE, 128), lambda i: (0, jnp.minimum(i, split_at - 1), 0)),
            pl.BlockSpec((4, WIDE, 128), lambda i: (0, jnp.maximum(i - split_at, 0), 0)),
            tile,
        ],
        out_specs=tile,
        out_shape=jax.ShapeDtypeStruct(slab.shape, slab.dtype),
        input_output_aliases={3: 0},
        compiler_params=PARAMS,
        cost_estimate=SMALL,
    )(z, other_low, other_high, slab)


def places(slab_rows, height, count):
    total = slab_rows.shape[0]
    kinds = total // count
    block_of = slab_rows // height
    member = (block_of[:, None] == jnp.arange(kinds)[None, :]).astype(jnp.float32).reshape(-1, 128, kinds)
    before = jnp.tril(jnp.ones((128, 128), jnp.float32), -1)
    within = jnp.einsum("ab,cbh->cah", before, member, preferred_element_type=jnp.float32)
    chunks = member.shape[0]
    sums = member.sum(1)
    ahead = jnp.dot(jnp.tril(jnp.ones((chunks, chunks), jnp.float32), -1), sums, preferred_element_type=jnp.float32)
    rank = ((within + ahead[:, None, :]) * member).sum(2).reshape(total)
    return block_of * count + rank.astype(jnp.int32)


def slab_weights(weights, slab_rows, x, zh, c, zl, cots, mode_vectors, cut):
    height = weights.shape[0]
    total = slab_rows.shape[0]
    count = total // 16
    harm = (x * 2 + zh) * 2 + c
    place = places(slab_rows, height, count)
    ids = harm * count + jnp.arange(count, dtype=jnp.int32)
    local_rows = jnp.where(place[None, :] == ids[:, None], slab_rows[None, :] - harm * height, 0).sum(1)
    own, below, above, far = ring_parts(jnp.take(weights, local_rows, axis=0, mode="clip"), ("zh", "zl"))
    near = jnp.concatenate([own, jnp.where(zl == 0, above, below)], axis=1)
    away = jnp.concatenate([far, jnp.where(zl == 0, below, above)], axis=1)
    pair, *pieces = with_pieces(jnp.stack([near, away]), mode_vectors, cut, cots[:1])
    ring = jnp.stack(ring_parts(pair, "x")).reshape(-1, 256)
    share = total // 64
    places_here = pick(place.reshape(4, 2, 4, 2, share).swapaxes(0, 1), zl)
    places_here = lax.dynamic_index_in_dim(places_here, x, 1, keepdims=False)

    def chosen(core):
        wanted = lax.dynamic_index_in_dim(places_here, core, 1, keepdims=False).reshape(-1)
        source, row = wanted // count, wanted % count
        source_x, source_zh, source_c = source // 4, (source // 2) % 2, source % 2
        number = (slot_of((source_x - x) % 4) * 2 + (source_zh != zh)) * count + row
        return number, source_c == c

    numbers, mine = zip(chosen(c), chosen(1 - c), strict=True)
    taken = jnp.take(ring, jnp.concatenate(numbers), axis=0, mode="clip")
    taken = jnp.where(jnp.concatenate(mine)[:, None], taken, 0.0).reshape(2, 4, share, 256)
    taken = released(taken, cots[1:])
    return taken[0] + shifted(taken[1], "c", 1), pieces


def slab_share(chosen, y):
    share = chosen.shape[1]
    came = jnp.stack(
        [
            pick(chosen, y),
            shifted(pick(chosen, (y + 1) % 4), "y", 1),
            shifted(pick(chosen, (y + 3) % 4), "y", -1),
            shifted(pick(chosen, (y + 2) % 4), "y", 2),
        ]
    )
    came = jnp.stack([pick(came, slot_of((k - y) % 4)) for k in range(4)])
    return came.reshape(4, share, 2, 128).transpose(1, 2, 0, 3).reshape(share, 1024)


def local(mode_vectors, weights, cotangent, eigenvalues, eigen_cotangent, slab_rows):
    x, zh, c, y, zl = (lax.axis_index(a) for a in ("x", "zh", "c", "y", "zl"))
    rows = mode_vectors.shape[0]
    cut = rows * 3 // 4
    own_x = lax.all_gather(mode_vectors, "y")
    early = rows // 4
    cots = (shifted(cotangent[:early], "zl", 1), shifted(cotangent[early:], "zl", 1))
    chosen, pieces = slab_weights(weights, slab_rows, x, zh, c, zl, cots, mode_vectors, cut)
    other_first, other_second = (shifted(piece, "zl", 1) for piece in pieces)
    share = slab_share(chosen, y)
    cot = cot_ready(cotangent, *cots)
    share = released(share, (other_first, cot))
    own_picked = lax.all_gather(share, "x")
    other_picked = shifted(own_picked, "c", 1)

    kept, sent, tail = gram_shares(cot, own_x, cut, (share,))
    to_self, to_above, to_below, to_far = x_parts(kept, shifted(sent, "c", 1), ())
    other_low = lax.all_gather(joined(other_first, other_second, (to_self,)), "y")
    total = to_self + shifted(to_above, "x", 1) + shifted(to_below, "x", -1) + shifted(to_far, "x", 2)
    own, below, above, far = ring_parts(total, ("zh", "zl"))
    total = jnp.concatenate([own + far, below + above], axis=1)
    j_first = (y * 2 + x // 2) * 128 + ((x % 2) * 2 + c) * 32
    eigen_j = lax.dynamic_slice_in_dim(eigenvalues, j_first, 32)
    slope_j = lax.dynamic_slice_in_dim(eigen_cotangent, j_first, 32)
    sides = eigenvalues.reshape(4, 2, 128).transpose(1, 0, 2).reshape(2, 512)
    eigen_i = jnp.where(zl == 0, sides, sides[::-1]).reshape(1024)
    differ = eigen_j[:, None] - eigen_i[None]
    factor = differ / (differ * differ + regular)
    j_ids = j_first + lax.broadcasted_iota(jnp.int32, (32, 1024), 0)
    col = lax.broadcasted_iota(jnp.int32, (32, 1024), 1)
    i_ids = (col % 512 // 128 * 2 + (zl + col // 512) % 2) * 128 + col % 128
    weighted = factor * total + jnp.where(j_ids == i_ids, slope_j[:, None], 0.0)

    other_high = shifted(released(tail, (weighted,)), "zl", 1)
    z_own = ring_parts(z_part(ring_parts(weighted, "y"), own_picked, other_picked), "x")
    z_other = [shifted(part, "c", 1) for part in z_own]
    z = z_ready(z_own, z_other)
    return slab_other(z, other_low, other_high, slab_own(z, own_x))


def solution(mesh):
    torus = Mesh(mesh.devices.reshape(4, 2, 2, 4, 2), ("x", "zh", "c", "y", "zl"))
    return jax.shard_map(
        local,
        mesh=torus,
        in_specs=(P(HARM, MODE), P(HARM, MODE), P(HARM, MODE), P(), P(), P()),
        out_specs=P(MODE, HARM),
        check_vma=False,
    )
```

```python
import jax
import jax.numpy as jnp
from jax import lax
from jax.experimental import pallas as pl
from jax.experimental.pallas import tpu as pltpu
from jax.sharding import Mesh
from jax.sharding import PartitionSpec as P

HARM = ("x", "zh", "c")
MODE = ("y", "zl")
SIZES = {"x": 4, "zh": 2, "c": 2, "y": 4, "zl": 2, ("zh", "zl"): 4}
regular = 0.01
TILE = 384
VMEM = 36 * 1024 * 1024


def shifted(array, axis, step):
    n = SIZES[axis]
    return lax.ppermute(array, axis, [(i, (i + step) % n) for i in range(n)])


def pick(parts, number):
    return lax.dynamic_index_in_dim(parts, number, 0, keepdims=False)


def slot_of(offset):
    return jnp.where(offset == 0, 0, jnp.where(offset == 3, 1, jnp.where(offset == 1, 2, 3)))


def ring_parts(array, axis):
    return [array, shifted(array, axis, 1), shifted(array, axis, -1), shifted(array, axis, 2)]


def split(value):
    high = value.astype(jnp.bfloat16)
    low = (value - high.astype(jnp.float32)).astype(jnp.bfloat16)
    return high, low


def three_pass(both, b, dims):
    high, low = b
    rows = both.shape[0] // 2

    def dot(p, q):
        return lax.dot_general(p, q, (dims, ((), ())), preferred_element_type=jnp.float32)

    first = dot(both, high)
    return first[:rows] + first[rows:] + dot(both[:rows], low)


SMALL = pl.CostEstimate(flops=1000, bytes_accessed=1000, transcendentals=0)
ANY = pl.BlockSpec(memory_space=pl.ANY)
STEP = 384
WIDE = 768
PARAMS = pltpu.CompilerParams(vmem_limit_bytes=VMEM)


def with_pieces(small, array, cut, after):
    rows = cut // 2

    def body(array_ref, small_ref, *refs):
        first, second = refs[-2:]
        step = pl.program_id(0)

        @pl.when(step == 0)
        def _():
            first[...] = array_ref[...]

        @pl.when(step == 1)
        def _():
            second[...] = array_ref[...]

    piece = jax.ShapeDtypeStruct((rows, 128), array.dtype)
    return pl.pallas_call(
        body,
        grid=(2,),
        in_specs=[pl.BlockSpec((rows, 128), lambda i: (i, 0)), ANY] + [ANY] * len(after),
        out_specs=[ANY] + [pl.BlockSpec((rows, 128), lambda i: (0, 0))] * 2,
        out_shape=[jax.ShapeDtypeStruct(small.shape, small.dtype), piece, piece],
        input_output_aliases={1: 0},
        compiler_params=PARAMS,
        cost_estimate=SMALL,
    )(array, small, *after)


def released(array, after):
    def body(*refs):
        pass

    return pl.pallas_call(
        body,
        in_specs=[ANY] * (1 + len(after)),
        out_specs=ANY,
        out_shape=jax.ShapeDtypeStruct(array.shape, array.dtype),
        input_output_aliases={0: 0},
        cost_estimate=SMALL,
    )(array, *after)


def x_parts(kept, came, after):
    def body(kept_ref, came_ref, *refs):
        x = lax.axis_index("x")
        for ref, offset in zip(refs[-4:], (0, 1, 3, 2), strict=True):
            share = lax.rem(x + offset, 4)
            ref[...] = kept_ref[share] + came_ref[share]

    return pl.pallas_call(
        body,
        in_specs=[pl.BlockSpec(kept.shape, lambda: (0, 0, 0))] * 2 + [ANY] * len(after),
        out_shape=[jax.ShapeDtypeStruct(kept.shape[1:], kept.dtype)] * 4,
        compiler_params=PARAMS,
        cost_estimate=SMALL,
    )(kept, came, *after)


def joined(first, second, after):
    rows = first.shape[0]

    def body(first_ref, second_ref, *refs):
        @pl.when(pl.program_id(0) == 0)
        def _():
            refs[-1][...] = first_ref[...]

        @pl.when(pl.program_id(0) == 1)
        def _():
            refs[-1][...] = second_ref[...]

    return pl.pallas_call(
        body,
        grid=(2,),
        in_specs=[pl.BlockSpec((rows, 128), lambda i: (0, 0))] * 2 + [ANY] * len(after),
        out_specs=pl.BlockSpec((rows, 128), lambda i: (i, 0)),
        out_shape=jax.ShapeDtypeStruct((2 * rows, 128), first.dtype),
        compiler_params=PARAMS,
        cost_estimate=SMALL,
    )(first, second, *after)


def cot_ready(own, first, second):
    rows = own.shape[0]
    split_at = first.shape[0] // STEP

    def body(own_ref, first_ref, second_ref, both):
        other = jnp.where(pl.program_id(0) < split_at, first_ref[...], second_ref[...])
        high, low = split(jnp.concatenate([own_ref[...].T, other.T], axis=0))
        both[:256], both[256:] = high, low

    return pl.pallas_call(
        body,
        grid=(rows // STEP,),
        in_specs=[
            pl.BlockSpec((STEP, 128), lambda i: (i, 0)),
            pl.BlockSpec((STEP, 128), lambda i: (jnp.minimum(i, split_at - 1), 0)),
            pl.BlockSpec((STEP, 128), lambda i: (jnp.maximum(i - split_at, 0), 0)),
        ],
        out_specs=pl.BlockSpec((512, STEP), lambda i: (0, i)),
        out_shape=jax.ShapeDtypeStruct((512, rows), jnp.bfloat16),
        compiler_params=PARAMS,
        cost_estimate=pl.CostEstimate(flops=1000, bytes_accessed=rows * 4096, transcendentals=0),
    )(own, first, second)


def wide(ref):
    return jnp.concatenate([ref[k] for k in range(4)], axis=1)


def gram_shares(cot, whole_x, cut, after):
    rows = whole_x.shape[1]
    step_rows = rows - cut
    steps, start = rows // step_rows, cut // step_rows

    def body(cot_ref, x_ref, *refs):
        kept, sent, tail, total = refs[-4:]
        step = pl.program_id(0)
        c, zl = lax.axis_index("c"), lax.axis_index("zl")

        @pl.when(step == 0)
        def _():
            total[...] = jnp.zeros_like(total)

        total[...] += three_pass(cot_ref[...], split(wide(x_ref)), ((1,), (0,)))

        @pl.when(step >= start)
        def _():
            tail[...] = x_ref[...]

        @pl.when(step == steps - 1)
        def _():
            for s in range(4):
                for ref, core in ((kept, c), (sent, 1 - c)):
                    row = pl.multiple_of(lax.rem(s * 64 + core * 32 + 128 * zl, 256), 32)
                    ref[s] = total[pl.ds(row, 32), :]

    shape = jax.ShapeDtypeStruct((4, 32, 512), jnp.float32)
    whole = pl.BlockSpec((4, 32, 512), lambda i: (0, 0, 0))
    return pl.pallas_call(
        body,
        grid=(steps,),
        in_specs=[pl.BlockSpec((512, step_rows), lambda i: (0, i))]
        + [pl.BlockSpec((4, step_rows, 128), lambda i: (0, i, 0))]
        + [ANY] * len(after),
        out_specs=[whole, whole, pl.BlockSpec((4, step_rows, 128), lambda i: (0, 0, 0))],
        out_shape=[shape, shape, jax.ShapeDtypeStruct((4, rows - cut, 128), jnp.float32)],
        scratch_shapes=[pltpu.VMEM((256, 512), jnp.float32)],
        compiler_params=PARAMS,
        cost_estimate=SMALL,
    )(cot, whole_x, *after)


def z_part(weighted, own, other):
    count, share, depth = own.shape

    def body(*refs):
        weighted_refs, own_ref, other_ref = refs[:4], refs[4], refs[5]
        out, tall, rows = refs[-3:]
        y, c = lax.axis_index("y"), lax.axis_index("c")
        for slot, offset in enumerate((0, 3, 1, 2)):
            tall[pl.ds(pl.multiple_of(lax.rem(y + offset, 4) * 32, 32), 32), :] = weighted_refs[slot][...]
        for k in range(count):
            for which, ref in ((c, own_ref), (1 - c, other_ref)):
                rows[pl.ds(pl.multiple_of((k * 2 + which) * share, share), share), :] = ref[k]
        out[...] = three_pass(jnp.concatenate(split(tall[...]), axis=0), split(rows[...]), ((1,), (1,)))

    return pl.pallas_call(
        body,
        out_shape=jax.ShapeDtypeStruct((128, 2 * count * share), jnp.float32),
        scratch_shapes=[pltpu.VMEM((128, depth), jnp.float32), pltpu.VMEM((2 * count * share, depth), jnp.float32)],
        compiler_params=PARAMS,
        cost_estimate=SMALL,
    )(*weighted, own, other)


def z_ready(own_z, other_z):
    depth, height = 1024, own_z[0].shape[1]

    def body(*refs):
        sets, (both, z_tall) = (refs[:4], refs[4:8]), refs[8:]
        x, c, zl = lax.axis_index("x"), lax.axis_index("c"), lax.axis_index("zl")
        for slot, offset in enumerate((0, 3, 1, 2)):
            source = lax.rem(x + offset, 4)
            side = lax.rem(source // 2 + zl, 2)
            for part in range(4):
                for which, held in ((c, sets[0]), (1 - c, sets[1])):
                    row = side * 512 + part * 128 + lax.rem(source, 2) * 64 + which * 32
                    z_tall[pl.ds(pl.multiple_of(row, 32), 32), :] = held[slot][part * 32 : part * 32 + 32, :]
        for part in range(depth // 128):
            cols = slice(part * 128, part * 128 + 128)
            both[:height, cols], both[height:, cols] = split(z_tall[cols, :].T)

    return pl.pallas_call(
        body,
        out_shape=jax.ShapeDtypeStruct((2 * height, depth), jnp.bfloat16),
        scratch_shapes=[pltpu.VMEM((depth, height), jnp.float32)],
        compiler_params=PARAMS,
        cost_estimate=SMALL,
    )(*own_z, *other_z)


def slab_own(z, own_x):
    total = own_x.shape[1]
    height, depth = z.shape[0] // 2, z.shape[1] // 2

    def body(z_ref, own_ref, out):
        out[...] = three_pass(z_ref[...], split(wide(own_ref)), ((1,), (1,)))

    return pl.pallas_call(
        body,
        grid=(total // WIDE,),
        in_specs=[
            pl.BlockSpec((2 * height, depth), lambda i: (0, 0)),
            pl.BlockSpec((4, WIDE, 128), lambda i: (0, i, 0)),
        ],
        out_specs=pl.BlockSpec((height, WIDE), lambda i: (0, i)),
        out_shape=jax.ShapeDtypeStruct((height, total), jnp.float32),
        compiler_params=PARAMS,
        cost_estimate=pl.CostEstimate(flops=1000, bytes_accessed=1 << 24, transcendentals=0),
    )(z, own_x)


def slab_other(z, other_low, other_high, slab):
    total = slab.shape[1]
    split_at = other_low.shape[1] // WIDE
    height, depth = z.shape[0] // 2, z.shape[1] // 2

    def body(z_ref, low_ref, high_ref, slab_ref, out):
        step = pl.program_id(0)

        def product(other_ref):
            out[...] = slab_ref[...] + three_pass(z_ref[...], split(wide(other_ref)), ((1,), (1,)))

        @pl.when(step < split_at)
        def _():
            product(low_ref)

        @pl.when(step >= split_at)
        def _():
            product(high_ref)

    tile = pl.BlockSpec((height, WIDE), lambda i: (0, i))
    return pl.pallas_call(
        body,
        grid=(total // WIDE,),
        in_specs=[
            pl.BlockSpec((2 * height, depth), lambda i: (0, 1)),
            pl.BlockSpec((4, WIDE, 128), lambda i: (0, jnp.minimum(i, split_at - 1), 0)),
            pl.BlockSpec((4, WIDE, 128), lambda i: (0, jnp.maximum(i - split_at, 0), 0)),
            tile,
        ],
        out_specs=tile,
        out_shape=jax.ShapeDtypeStruct(slab.shape, slab.dtype),
        input_output_aliases={3: 0},
        compiler_params=PARAMS,
        cost_estimate=SMALL,
    )(z, other_low, other_high, slab)


def places(slab_rows, height, count):
    total = slab_rows.shape[0]
    kinds = total // count
    block_of = slab_rows // height
    member = (block_of[:, None] == jnp.arange(kinds)[None, :]).astype(jnp.float32).reshape(-1, 128, kinds)
    before = jnp.tril(jnp.ones((128, 128), jnp.float32), -1)
    within = jnp.einsum("ab,cbh->cah", before, member, preferred_element_type=jnp.float32)
    chunks = member.shape[0]
    sums = member.sum(1)
    ahead = jnp.dot(jnp.tril(jnp.ones((chunks, chunks), jnp.float32), -1), sums, preferred_element_type=jnp.float32)
    rank = ((within + ahead[:, None, :]) * member).sum(2).reshape(total)
    return block_of * count + rank.astype(jnp.int32)


def slab_weights(weights, slab_rows, x, zh, c, zl, cots, mode_vectors, cut):
    height = weights.shape[0]
    total = slab_rows.shape[0]
    count = total // 16
    harm = (x * 2 + zh) * 2 + c
    place = places(slab_rows, height, count)
    ids = harm * count + jnp.arange(count, dtype=jnp.int32)
    local_rows = jnp.where(place[None, :] == ids[:, None], slab_rows[None, :] - harm * height, 0).sum(1)
    own, below, above, far = ring_parts(jnp.take(weights, local_rows, axis=0, mode="clip"), ("zh", "zl"))
    near = jnp.concatenate([own, jnp.where(zl == 0, above, below)], axis=1)
    away = jnp.concatenate([far, jnp.where(zl == 0, below, above)], axis=1)
    pair, *pieces = with_pieces(jnp.stack([near, away]), mode_vectors, cut, cots[:1])
    ring = jnp.stack(ring_parts(pair, "x")).reshape(-1, 256)
    share = total // 64
    places_here = pick(place.reshape(4, 2, 4, 2, share).swapaxes(0, 1), zl)
    places_here = lax.dynamic_index_in_dim(places_here, x, 1, keepdims=False)

    def chosen(core):
        wanted = lax.dynamic_index_in_dim(places_here, core, 1, keepdims=False).reshape(-1)
        source, row = wanted // count, wanted % count
        source_x, source_zh, source_c = source // 4, (source // 2) % 2, source % 2
        number = (slot_of((source_x - x) % 4) * 2 + (source_zh != zh)) * count + row
        return number, source_c == c

    numbers, mine = zip(chosen(c), chosen(1 - c), strict=True)
    taken = jnp.take(ring, jnp.concatenate(numbers), axis=0, mode="clip")
    taken = jnp.where(jnp.concatenate(mine)[:, None], taken, 0.0).reshape(2, 4, share, 256)
    taken = released(taken, cots[1:])
    return taken[0] + shifted(taken[1], "c", 1), pieces


def slab_share(chosen, y):
    share = chosen.shape[1]
    came = jnp.stack(
        [
            pick(chosen, y),
            shifted(pick(chosen, (y + 1) % 4), "y", 1),
            shifted(pick(chosen, (y + 3) % 4), "y", -1),
            shifted(pick(chosen, (y + 2) % 4), "y", 2),
        ]
    )
    came = jnp.stack([pick(came, slot_of((k - y) % 4)) for k in range(4)])
    return came.reshape(4, share, 2, 128).transpose(1, 2, 0, 3).reshape(share, 1024)


def local(mode_vectors, weights, cotangent, eigenvalues, eigen_cotangent, slab_rows):
    x, zh, c, y, zl = (lax.axis_index(a) for a in ("x", "zh", "c", "y", "zl"))
    rows = mode_vectors.shape[0]
    cut = rows * 3 // 4
    own_x = lax.all_gather(mode_vectors, "y")
    early = rows // 4
    cots = (shifted(cotangent[:early], "zl", 1), shifted(cotangent[early:], "zl", 1))
    chosen, pieces = slab_weights(weights, slab_rows, x, zh, c, zl, cots, mode_vectors, cut)
    other_first, other_second = (shifted(piece, "zl", 1) for piece in pieces)
    share = slab_share(chosen, y)
    cot = cot_ready(cotangent, *cots)
    share = released(share, (other_first, cot))
    own_picked = lax.all_gather(share, "x")
    other_picked = shifted(own_picked, "c", 1)

    kept, sent, tail = gram_shares(cot, own_x, cut, (share,))
    to_self, to_above, to_below, to_far = x_parts(kept, shifted(sent, "c", 1), ())
    other_low = lax.all_gather(joined(other_first, other_second, (to_self,)), "y")
    total = to_self + shifted(to_above, "x", 1) + shifted(to_below, "x", -1) + shifted(to_far, "x", 2)
    own, below, above, far = ring_parts(total, ("zh", "zl"))
    total = jnp.concatenate([own + far, below + above], axis=1)
    j_first = (y * 2 + x // 2) * 128 + ((x % 2) * 2 + c) * 32
    eigen_j = lax.dynamic_slice_in_dim(eigenvalues, j_first, 32)
    slope_j = lax.dynamic_slice_in_dim(eigen_cotangent, j_first, 32)
    sides = eigenvalues.reshape(4, 2, 128).transpose(1, 0, 2).reshape(2, 512)
    eigen_i = jnp.where(zl == 0, sides, sides[::-1]).reshape(1024)
    differ = eigen_j[:, None] - eigen_i[None]
    factor = differ / (differ * differ + regular)
    j_ids = j_first + lax.broadcasted_iota(jnp.int32, (32, 1024), 0)
    col = lax.broadcasted_iota(jnp.int32, (32, 1024), 1)
    i_ids = (col % 512 // 128 * 2 + (zl + col // 512) % 2) * 128 + col % 128
    weighted = factor * total + jnp.where(j_ids == i_ids, slope_j[:, None], 0.0)

    other_high = shifted(released(tail, (weighted,)), "zl", 1)
    z_own = ring_parts(z_part(ring_parts(weighted, "y"), own_picked, other_picked), "x")
    z_other = [shifted(part, "c", 1) for part in z_own]
    z = z_ready(z_own, z_other)
    return slab_other(z, other_low, other_high, slab_own(z, own_x))


def solution(mesh):
    torus = Mesh(mesh.devices.reshape(4, 2, 2, 4, 2), ("x", "zh", "c", "y", "zl"))
    return jax.shard_map(
        local,
        mesh=torus,
        in_specs=(P(HARM, MODE), P(HARM, MODE), P(HARM, MODE), P(), P(), P()),
        out_specs=P(MODE, HARM),
        check_vma=False,
    )
```
